128 devices in a mesh: seq: 16 (over y, z_lo, core), tp: 4 (over x), rep: 2 (over z_hi).
Axes of the slice: x: 4, y: 4, z: 4 (z_hi: 2, z_lo: 2; z = z_hi * 2 + z_lo), core: 2. Of those that a mesh axis runs over, the one named last changes fastest.
Arguments:
- tokens: bfloat16 [2, 12288, 3072], P('rep', 'seq'), may hold values from -6 to 6
- in_panels: bfloat16 [3072, 4, 4096], P(('seq', 'rep'), None, 'tp'), may hold values from -0.109375 to 0.109375
- out_panel: bfloat16 [4096, 3072], P('tp', ('seq', 'rep')), may hold values from -0.09375 to 0.09375
- decay_power: int32 [32], P('tp'), may hold values from 0 to 8
- boundary: int32 [2], P('rep'), may hold values from 1 to 12287
Outputs:
- layer_out: bfloat16 [2, 12288, 3072], P('rep', 'seq', 'tp')
The draws below stay inside these ranges and needn't reach their ends.
All inputs are finite; a program needn't handle non-finite values.
Results may differ from the reference program's by a relative error of at most 0.019.
Values may be sent and summed in bfloat16 or wider, within the bound.
A program may use at most 128 MiB of HBM per device.

```python
import jax
import jax.numpy as jnp
from jax import lax

D = 3072
HEADS = 32
HDIM = 128
BLK = 768
TOKENS = 12288
N_TP = 4
N_REP = 2


def with_ends(drawn, key, low, top_value):
    place = [jax.random.randint(jax.random.fold_in(key, axis), (), 0, length) for axis, length in enumerate(drawn.shape)]
    main_axis = drawn.shape.index(max(drawn.shape))
    beside = place[:main_axis] + [(place[main_axis] + 1) % drawn.shape[main_axis]] + place[main_axis + 1:]
    return drawn.at[tuple(place)].set(low).at[tuple(beside)].set(top_value)


def level_of(key, dims, shards, smallest, high):
    def one(axis_at, parts):
        draws = jax.random.uniform(jax.random.fold_in(jax.random.fold_in(key, 6), axis_at), (parts,), jnp.float32, smallest / len(shards), high / len(shards))
        return jnp.repeat(jnp.exp(draws), dims[axis_at] // parts).reshape((-1,) + (1,) * (len(dims) - axis_at - 1))

    loudness = one(*shards[0])
    for cut in shards[1:]:
        loudness = loudness * one(*cut)
    return loudness


def noise(own_key, shape, spread, most, cuts=(), kind=jnp.bfloat16):
    values = jax.random.normal(own_key, shape, jnp.float32) * spread
    if len(cuts) > 0:
        values = level_of(own_key, shape, cuts, -0.22, 0.18) * values
    return jnp.clip(values, min=-most, max=most).astype(kind)


def setup_inputs(seed: int = 0) -> dict:
    seeds = jax.random.split(jax.random.key(seed), 6)
    return {
        "tokens": noise(seeds[0], (N_REP, TOKENS, D), 1.0, 6.0, ((0, 2), (1, 16))),
        "in_panels": noise(seeds[1], (D, 4, HEADS * HDIM), D ** -0.5, 0.109375, ((0, 32), (2, 4))),
        "out_panel": noise(seeds[2], (HEADS * HDIM, D), (HEADS * HDIM) ** -0.5, 0.09375, ((0, 4), (1, 32))),
        "decay_power": with_ends(jax.random.randint(seeds[3], (HEADS,), 0, 9), jax.random.fold_in(seeds[3], 1), 0, 8).astype(jnp.int32),
        "boundary": jax.random.randint(seeds[4], (N_REP,), 1, TOKENS).astype(jnp.int32),
    }


log_half = -0.6931471805599453
epsilon = 1e-06

def attend_block(queries, key_rows, val_rows, state_in, log_rate, anchor, prompt_start):
    extent = queries.shape[0]
    positions = anchor + jnp.arange(extent, dtype=jnp.int32)
    newer_mask = positions >= prompt_start
    offsets = (positions[:, None] - positions[None, :]).astype(jnp.float32)
    allowed = (offsets >= 0.0) & (newer_mask[:, None] == newer_mask[None, :])
    weights = jnp.where(allowed[None], jnp.exp(log_rate[:, None, None] * jnp.maximum(offsets, 0.0)[None]), 0.0)
    scores = jnp.einsum('ihd,jhd->hij', queries.astype(jnp.float32), key_rows.astype(jnp.float32), precision=lax.Precision.HIGHEST)
    scores = (scores * weights).astype(jnp.bfloat16)
    within = jnp.einsum('hij,jhd->ihd', scores.astype(jnp.float32), val_rows.astype(jnp.float32), precision=lax.Precision.HIGHEST)
    use_prior = ((positions < prompt_start) | (anchor > prompt_start)).astype(jnp.float32)
    steps_in = (positions - anchor + 1).astype(jnp.float32)
    query_scale = jnp.exp(log_rate[None, :] * steps_in[:, None]) * use_prior[:, None]
    scaled = queries.astype(jnp.float32) * query_scale[:, :, None]
    across = jnp.einsum('ihd,hde->ihe', scaled, state_in, precision=lax.Precision.HIGHEST)
    final_pos = anchor + extent - 1
    kept_rows = (newer_mask == (final_pos >= prompt_start)).astype(jnp.float32)
    steps_out = (final_pos - positions).astype(jnp.float32)
    key_scale = jnp.exp(log_rate[None, :] * steps_out[:, None]) * kept_rows[:, None]
    decayed = (key_rows.astype(jnp.float32) * key_scale[:, :, None]).astype(jnp.bfloat16)
    local_state = jnp.einsum('jhd,jhe->hde', decayed.astype(jnp.float32), val_rows.astype(jnp.float32), precision=lax.Precision.HIGHEST)
    crossed = (anchor <= prompt_start) & (prompt_start <= final_pos)
    passing = jnp.exp(log_rate * extent) * jnp.where(crossed, 0.0, 1.0).astype(jnp.float32)
    return (within + across, local_state, passing)

def reference(tokens, in_panels, out_panel, decay_power, boundary):
    log_rate = log_half * jnp.exp2(decay_power.astype(jnp.float32)) / TOKENS
    flat_panels = in_panels.reshape(D, 4 * HEADS * HDIM)
    group_width = HEADS * HDIM // N_TP
    results = []
    for replica in range(N_REP):
        slab_rows = tokens[replica].reshape(TOKENS // BLK, BLK, D)
        prompt_start = boundary[replica]

        def advance(state, packed):
            rows_in, number = packed
            anchor = number * BLK
            projected = jnp.dot(rows_in, flat_panels, preferred_element_type=jnp.float32).reshape(BLK, 4, HEADS, HDIM)
            queries = (jax.nn.silu(projected[:, 0]) * HDIM ** (-0.5)).astype(jnp.bfloat16)
            key_rows = jax.nn.silu(projected[:, 1]).astype(jnp.bfloat16)
            val_rows = projected[:, 2].astype(jnp.bfloat16)
            gate_rows = jax.nn.sigmoid(projected[:, 3])
            attended, local_state, passing = attend_block(queries, key_rows, val_rows, state, log_rate, anchor, prompt_start)
            new_state = passing[:, None, None] * state + local_state
            square = lax.optimization_barrier(jnp.mean(attended * attended, axis=-1, keepdims=True))
            gated_rows = (attended * lax.rsqrt(square + epsilon) * gate_rows).astype(jnp.bfloat16).reshape(BLK, HEADS * HDIM)
            summed = jnp.zeros((BLK, D), jnp.float32)
            for column_group in range(N_TP):
                lower = column_group * group_width
                head_partial = jnp.dot(gated_rows[:, lower:lower + group_width], out_panel[lower:lower + group_width], preferred_element_type=jnp.float32)
                rounded = lax.optimization_barrier(head_partial.astype(jnp.bfloat16))
                summed = summed + rounded.astype(jnp.float32)
            return (new_state, summed.astype(jnp.bfloat16))
        start_state = jnp.zeros((HEADS, HDIM, HDIM), jnp.float32)
        numbers = jnp.arange(TOKENS // BLK, dtype=jnp.int32)
        final_state, blocks = lax.scan(advance, start_state, (slab_rows, numbers))
        results.append(blocks.reshape(TOKENS, D))
    return jnp.stack(results)
```

```python
import jax
import jax.numpy as jnp
from jax import lax
from jax.sharding import PartitionSpec as P

D = 3072
HDIM = 128


log_half = -0.6931471805599453
epsilon = 1e-06


def attend_block(queries, key_rows, val_rows, log_rate, anchor, prompt_start):
    extent = queries.shape[0]
    positions = anchor + jnp.arange(extent, dtype=jnp.int32)
    newer_mask = positions >= prompt_start
    offsets = (positions[:, None] - positions[None, :]).astype(jnp.float32)
    allowed = (offsets >= 0.0) & (newer_mask[:, None] == newer_mask[None, :])
    weights = jnp.where(
        allowed[None], jnp.exp(log_rate[:, None, None] * jnp.maximum(offsets, 0.0)[None]), 0.0
    )
    scores = jnp.einsum("ihd,jhd->hij", queries, key_rows, preferred_element_type=jnp.float32)
    scores = (scores * weights).astype(jnp.bfloat16)
    within = jnp.einsum("hij,jhd->ihd", scores, val_rows, preferred_element_type=jnp.float32)
    final_pos = anchor + extent - 1
    kept_rows = (newer_mask == (final_pos >= prompt_start)).astype(jnp.float32)
    steps_out = (final_pos - positions).astype(jnp.float32)
    key_scale = jnp.exp(log_rate[None, :] * steps_out[:, None]) * kept_rows[:, None]
    decayed = (key_rows.astype(jnp.float32) * key_scale[:, :, None]).astype(jnp.bfloat16)
    local_state = jnp.einsum("jhd,jhe->hde", decayed, val_rows, preferred_element_type=jnp.float32)
    return within, local_state


def local(tokens, in_panels, out_panel, decay_power, boundary):
    slab_rows = tokens[0]
    extent = slab_rows.shape[0]
    seq_count = lax.axis_size("seq")
    own_index = lax.axis_index("seq")
    anchor = own_index * extent
    prompt_start = boundary[0]
    log_rate = log_half * jnp.exp2(decay_power.astype(jnp.float32)) / (extent * seq_count)
    head_count = decay_power.shape[0]
    width = in_panels.shape[2]
    flat_in = lax.optimization_barrier(in_panels.reshape(in_panels.shape[0], 4 * width))
    full_in = lax.all_gather(flat_in, ("seq", "rep"), axis=0, tiled=True)
    full_out = lax.all_gather(out_panel.T, ("seq", "rep"), axis=0, tiled=True)
    projected = jnp.dot(slab_rows, full_in, preferred_element_type=jnp.float32)
    projected = lax.optimization_barrier(projected)
    projected = projected.reshape(extent, 4, head_count, HDIM)
    queries = (jax.nn.silu(projected[:, 0]) * HDIM ** (-0.5)).astype(jnp.bfloat16)
    key_rows = jax.nn.silu(projected[:, 1]).astype(jnp.bfloat16)
    val_rows = projected[:, 2].astype(jnp.bfloat16)
    gate_rows = jax.nn.sigmoid(projected[:, 3])
    within, local_state = attend_block(
        queries, key_rows, val_rows, log_rate, anchor, prompt_start
    )
    states = lax.all_gather(local_state.astype(jnp.bfloat16), "seq")
    owners = jnp.arange(seq_count, dtype=jnp.int32)
    between = (own_index - 1 - owners).astype(jnp.float32)
    crossing = prompt_start // extent
    reaches = (owners < own_index) & ~((owners < crossing) & (crossing < own_index))
    carry = jnp.where(
        reaches[:, None],
        jnp.exp(log_rate[None, :] * extent * jnp.maximum(between, 0.0)[:, None]),
        0.0,
    )
    prior_state = jnp.sum(carry[:, :, None, None] * states.astype(jnp.float32), axis=0)
    attended = within
    positions = anchor + jnp.arange(extent, dtype=jnp.int32)
    use_prior = ((positions < prompt_start) | (anchor > prompt_start)).astype(jnp.float32)
    steps_in = jnp.arange(1, extent + 1, dtype=jnp.int32).astype(jnp.float32)
    query_scale = jnp.exp(log_rate[None, :] * steps_in[:, None]) * use_prior[:, None]
    scaled = queries.astype(jnp.float32) * query_scale[:, :, None]
    attended = attended + jnp.einsum(
        "ihd,hde->ihe", scaled, prior_state, precision=lax.Precision.HIGHEST
    )
    square = jnp.mean(attended * attended, axis=-1, keepdims=True)
    gated_rows = (
        (attended * lax.rsqrt(square + epsilon) * gate_rows)
        .astype(jnp.bfloat16)
        .reshape(extent, head_count * HDIM)
    )
    head_partial = lax.dot_general(
        gated_rows, full_out, (((1,), (1,)), ((), ())), preferred_element_type=jnp.float32
    )
    summed = lax.psum_scatter(
        head_partial.astype(jnp.bfloat16), "tp", scatter_dimension=1, tiled=True
    )
    return summed[None]


def solution(mesh):
    return jax.shard_map(
        local,
        mesh=mesh,
        in_specs=(
            P("rep", "seq", None),
            P(("seq", "rep"), None, "tp"),
            P("tp", ("seq", "rep")),
            P("tp"),
            P("rep"),
        ),
        out_specs=P("rep", "seq", "tp"),
        check_vma=False,
    )
```

```python
import functools

import jax
import jax.numpy as jnp
from jax import lax
from jax.experimental import pallas as pl
from jax.experimental.pallas import tpu as pltpu
from jax.sharding import PartitionSpec as P

HDIM = 128
MESH = pl.DeviceIdType.MESH
log_half = -0.6931471805599453
epsilon = 1e-06
F32 = jnp.float32
BF16 = jnp.bfloat16


def nt_dot(a, b):
    return lax.dot_general(a, b, (((1,), (1,)), ((), ())), preferred_element_type=F32)


def tn_dot(a, b):
    return lax.dot_general(a, b, (((0,), (0,)), ((), ())), preferred_element_type=F32)


def kernel(
    heads, rates, coef, place, tok, wsh, osh, out,
    G, tokv, gall, qbuf, wbuf, gbuf, pbuf, lbuf, tbuf, acc,
    loc, s1, r1, s2, r2, ssib, rsib, sa, ra, sl, rl, st, rt, sx, rx,
):
    extent = tok.shape[0]
    rows = wsh.shape[2]
    half = rows // 2
    steps = heads + 2
    pieces = steps // 2
    rem, div = lax.rem, lax.div
    s, x, zhi = lax.axis_index("seq"), lax.axis_index("tp"), lax.axis_index("rep")
    y, g, zlo, c = div(s, 4), rem(s, 4), rem(div(s, 2), 2), rem(s, 2)
    z = zhi * 2 + zlo

    def around(k, d):
        return rem(k + d, 4)

    def at_y(k):
        return {"seq": k * 4 + g}

    def at_z(k):
        return {"seq": y * 4 + rem(k, 2) * 2 + c, "rep": div(k, 2)}

    def at_g(k):
        return {"seq": y * 4 + k}

    def at_x(k):
        return {"tp": k}

    sibling = {"seq": y * 4 + zlo * 2 + 1 - c}

    def dest(q):
        return {"tp": y, "seq": q * 4 + g}

    def source(k):
        return {"tp": k, "seq": x * 4 + g}

    corner = x == y

    barrier = pltpu.get_barrier_semaphore()

    def greet(device):
        pl.semaphore_signal(barrier, inc=1, device_id=device, device_id_type=MESH)

    own_copies = [
        pltpu.make_async_copy(tok, tokv, loc.at[0]),
        pltpu.make_async_copy(wsh, G.at[pl.ds(0, heads), :, y, zlo, c, zhi], loc.at[1]),
    ]
    own_copies[1].start()
    for d in (1, 2, 3):
        greet(at_y(around(y, d)))
        greet(at_g(around(g, d)))
    for d in (1, 3):
        greet(at_z(around(z, d)))
        greet(at_x(around(x, d)))
    for k in range(4):
        @pl.when(jnp.logical_not(corner & (y == k)))
        def _():
            greet(dest(k))
        @pl.when(jnp.logical_not(corner & (x == k)))
        def _():
            greet(source(k))
    pl.semaphore_wait(barrier, 10 + jnp.where(corner, 6, 8))

    def send(src, dst, ss, rs, device):
        pltpu.make_async_remote_copy(
            src_ref=src, dst_ref=dst, send_sem=ss, recv_sem=rs, device_id=device, device_id_type=MESH
        ).start()

    def got(ref, ss, rs):
        pltpu.make_async_remote_copy(
            src_ref=ref, dst_ref=ref, send_sem=ss, recv_sem=rs, device_id=sibling, device_id_type=MESH
        ).wait_recv()

    def sent(ref, ss, rs):
        pltpu.make_async_remote_copy(
            src_ref=ref, dst_ref=ref, send_sem=ss, recv_sem=rs, device_id=sibling, device_id_type=MESH
        ).wait_send()

    first_ring = ((y, at_y), (z, at_z))
    second_ring = ((z, at_z), (y, at_y))

    def unit1(m, a, k, lo=0, n=rows):
        if a == 0:
            return G.at[pl.ds(2 * m, 2), 0, k, zlo, c, zhi, pl.ds(lo, n)]
        return G.at[pl.ds(2 * m, 2), 1, y, rem(k, 2), c, div(k, 2), pl.ds(lo, n)]

    def unit2(t, a, k):
        if a == 0:
            return G.at[t, 0, :, rem(k, 2), c, div(k, 2)]
        return G.at[t, 1, k, :, c]

    def half2(t, a, k, part):
        if a == 0:
            return G.at[t, 0, pl.ds(2 * part, 2), rem(k, 2), c, div(k, 2)]
        return G.at[t, 1, k, pl.ds(part, 1), c]

    def first_send(m):
        for a in (0, 1):
            k, at = first_ring[a]
            own = unit1(m, a, k)
            for d, step in ((0, 1), (1, 3)):
                send(own, own, s1.at[m, a, d], r1.at[m, a, d], at(around(k, step)))

    def first_pass(m):
        for a in (0, 1):
            k, at = first_ring[a]
            for d, step in ((0, 1), (1, 3)):
                origin = around(k, 4 - step)
                got(unit1(m, a, origin), s1.at[m, a, d], r1.at[m, a, d])
                part = unit1(m, a, origin, d * half, half)
                send(part, part, s1.at[m, a, 2 + d], r1.at[m, a, 2 + d], at(around(k, step)))

    def first_end(m):
        for a in (0, 1):
            k, _ = first_ring[a]
            for d in (0, 1):
                part = unit1(m, a, around(k, 2), d * half, half)
                got(part, s1.at[m, a, 2 + d], r1.at[m, a, 2 + d])

    def second_send(t):
        for a in (1, 0):
            k, at = second_ring[a]
            own = unit2(t, a, k)
            for d, step in ((0, 1), (1, 3)):
                send(own, own, s2.at[t, a, d], r2.at[t, a, d], at(around(k, step)))

    def second_pass(t):
        for a in (1, 0):
            k, at = second_ring[a]
            for d, step in ((0, 1), (1, 3)):
                origin = around(k, 4 - step)
                got(unit2(t, a, origin), s2.at[t, a, d], r2.at[t, a, d])
                part = half2(t, a, origin, d)
                send(part, part, s2.at[t, a, 2 + d], r2.at[t, a, 2 + d], at(around(k, step)))

    def second_end(t):
        for a in (1, 0):
            k, _ = second_ring[a]
            for d in (0, 1):
                got(half2(t, a, around(k, 2), d), s2.at[t, a, 2 + d], r2.at[t, a, 2 + d])

    def share(t):
        mine = G.at[t, :, :, :, c]
        send(mine, mine, ssib.at[t], rsib.at[t], sibling)

    def shared(t):
        got(G.at[t, :, :, :, 1 - c], ssib.at[t], rsib.at[t])

    def out_unit(k, q):
        return G.at[heads + div(k, 2), rem(k, 2), q, zlo, c, zhi]

    own_copies[1].wait()
    first_send(0)
    first_send(1)
    for q in range(4):
        width = osh.shape[1] // 4
        columns = osh.at[:, pl.ds(q * width, width)]
        is_own = corner & (y == q)
        @pl.when(is_own)
        def _():
            pltpu.make_async_copy(columns, out_unit(x, q), loc.at[2]).start()
        @pl.when(jnp.logical_not(is_own))
        def _():
            send(columns, out_unit(x, q), sa.at[q], ra.at[x], dest(q))
    own_copies[0].start()
    first_pass(0)
    first_send(2)
    first_pass(1)
    first_end(0)
    second_send(0)
    second_send(1)
    first_pass(2)
    first_end(1)
    second_send(2)
    first_send(3)
    own_copies[0].wait()
    second_pass(0)
    for k in range(4):
        is_own = corner & (x == k)
        @pl.when(is_own)
        def _():
            pltpu.make_async_copy(osh.at[:, pl.ds(0, osh.shape[1] // 4)], out_unit(k, y), loc.at[2]).wait()
        @pl.when(jnp.logical_not(is_own))
        def _():
            got(out_unit(k, y), sa.at[k], ra.at[k])
    acc[...] = jnp.zeros_like(acc)

    edge = place[0]
    down = lax.broadcasted_iota(jnp.int32, (extent, HDIM), 0)
    BR = 256

    def project(h):
        slot = rem(h, 4)
        rate = rates[h]
        panel = G[h, 0].reshape(-1, 2 * HDIM)
        u = jnp.dot(tokv[...], panel, preferred_element_type=F32)
        down_f = down.astype(F32)
        grow = jnp.exp(rate * down_f)
        shrink = jnp.exp(-rate * down_f)
        uq, uk = u[:, :HDIM], u[:, HDIM:]
        q = ((uq / (1.0 + jnp.exp(-uq))) * (HDIM ** -0.5) * grow).astype(BF16)
        kf = (uk / (1.0 + jnp.exp(-uk))) * shrink
        k = kf.astype(BF16)
        kept = jnp.where((down >= edge) | (edge >= extent), kf, 0.0).astype(BF16)
        panel = G[h, 1].reshape(-1, 2 * HDIM)
        u = jnp.dot(tokv[...], panel, preferred_element_type=F32)
        v = u[:, :HDIM].astype(BF16)
        gbuf[slot] = 1.0 / (1.0 + jnp.exp(-u[:, HDIM:]))
        qbuf[slot] = q
        lbuf[h, g] = (tn_dot(kept, v) * coef[h, 13]).astype(BF16)
        for d in (1, 2, 3):
            own = lbuf.at[h, g]
            send(own, own, sl.at[h, d - 1], rl.at[h, d - 1], at_g(around(g, d)))
        for lo in range(0, extent, BR):
            hi = lo + BR
            scores = nt_dot(q[lo:hi], k[:hi])
            i = lax.broadcasted_iota(jnp.int32, (BR, hi), 0) + lo
            j = lax.broadcasted_iota(jnp.int32, (BR, hi), 1)
            keep = (j <= i) & (j >= jnp.where(i >= edge, edge, 0))
            scores = jnp.where(keep, scores, 0.0).astype(BF16)
            wbuf[slot, pl.ds(lo, BR)] = jnp.dot(scores, v[:hi], preferred_element_type=F32)

    def gather_states(h):
        for d in (1, 2, 3):
            got(lbuf.at[h, around(g, 4 - d)], sl.at[h, d - 1], rl.at[h, d - 1])
        total = jnp.zeros((HDIM, HDIM), F32)
        before = jnp.zeros((HDIM, HDIM), F32)
        for k in range(4):
            part = lbuf[h, k].astype(F32)
            total += coef[h, k] * part
            before += coef[h, 4 + k] * part
        pbuf[rem(h, 4)] = before
        tbuf[h, y] = total.astype(BF16)
        for d in (1, 2, 3):
            own = tbuf.at[h, y]
            send(own, own, st.at[h, d - 1], rt.at[h, d - 1], at_y(around(y, d)))

    def finish(h):
        slot = rem(h, 4)
        for d in (1, 2, 3):
            got(tbuf.at[h, around(y, 4 - d)], st.at[h, d - 1], rt.at[h, d - 1])
        state = pbuf[slot]
        for k in range(4):
            state += coef[h, 8 + k] * tbuf[h, k].astype(F32)
        use = jnp.where((down < edge) | (edge < 0), coef[h, 12], 0.0)
        across = jnp.dot(qbuf[slot], state.astype(BF16), preferred_element_type=F32)
        attended = wbuf[slot] + across * use
        square = jnp.mean(attended * attended, axis=-1, keepdims=True)
        gall[x, h] = (attended * lax.rsqrt(square + epsilon) * gbuf[slot]).astype(BF16)
        own = gall.at[x, h]
        for d, step in ((0, 1), (1, 3)):
            send(own, own, sx.at[h, d], rx.at[h, d], at_x(around(x, step)))

    def half_rows(k, h, d):
        return gall.at[k, h, pl.ds(d * (extent // 2), extent // 2)]

    def pass_gated(h):
        for d, step in ((0, 1), (1, 3)):
            origin = around(x, 4 - step)
            got(gall.at[origin, h], sx.at[h, d], rx.at[h, d])
            part = half_rows(origin, h, d)
            send(part, part, sx.at[h, 2 + d], rx.at[h, 2 + d], at_x(around(x, step)))

    def end_gated(h):
        for d in (0, 1):
            got(half_rows(around(x, 2), h, d), sx.at[h, 2 + d], rx.at[h, 2 + d])

    def emit(i, q):
        panel = jnp.concatenate(
            [G[heads + i, a, q].reshape(-1, 2 * HDIM) for a in (0, 1)], axis=1
        )
        for lo in range(0, extent, BR):
            left = jnp.concatenate(
                [gall[2 * i + a, 2 * q + b, pl.ds(lo, BR)] for a in (0, 1) for b in (0, 1)], axis=1
            )
            acc[pl.ds(lo, BR)] += nt_dot(left, panel)

    def turn(t, carry):
        odd = rem(t, 2) == 1
        @pl.when(odd & (t <= 5))
        def _():
            first_end(div(t + 3, 2))
        @pl.when(odd & (t <= 3))
        def _():
            first_pass(div(t + 5, 2))
        @pl.when(t == 1)
        def _():
            first_send(4)
        @pl.when(t + 3 < steps)
        def _():
            second_send(t + 3)
        @pl.when(t + 1 < steps)
        def _():
            second_pass(t + 1)
        @pl.when((t >= 1) & (t - 1 < steps))
        def _():
            second_end(t - 1)
            share(t - 1)
        @pl.when((t >= 5) & (t - 5 < heads))
        def _():
            pass_gated(t - 5)
        @pl.when((t >= 4) & (t - 4 < heads))
        def _():
            finish(t - 4)
        @pl.when((t >= 3) & (t - 3 < heads))
        def _():
            gather_states(t - 3)
        @pl.when((t >= 2) & (t - 2 < steps))
        def _():
            shared(t - 2)
        @pl.when((t >= 2) & (t - 2 < heads))
        def _():
            project(t - 2)
        @pl.when((t >= 6) & (t - 6 < heads))
        def _():
            end_gated(t - 6)
        @pl.when(t >= heads + 2)
        def _():
            i = t - heads - 2
            def add(q, carry):
                emit(i, q)
                return carry
            lax.fori_loop(0, 2, add, 0)
        return carry

    lax.fori_loop(0, steps + 2, turn, 0)
    pass_gated(heads - 1)
    end_gated(heads - 2)
    lax.fori_loop(0, 2, lambda i, carry: (emit(i, 2), carry)[1], 0)
    end_gated(heads - 1)
    lax.fori_loop(0, 2, lambda i, carry: (emit(i, 3), carry)[1], 0)
    out[...] = acc[...].astype(out.dtype)

    def drain1(m, carry):
        for a in (0, 1):
            k, _ = first_ring[a]
            for d in (0, 1):
                sent(unit1(m, a, k), s1.at[m, a, d], r1.at[m, a, d])
                sent(unit1(m, a, k, 0, half), s1.at[m, a, 2 + d], r1.at[m, a, 2 + d])
        return carry

    def drain2(t, carry):
        for a in (0, 1):
            k, _ = second_ring[a]
            for d in (0, 1):
                sent(unit2(t, a, k), s2.at[t, a, d], r2.at[t, a, d])
                sent(half2(t, a, k, 0), s2.at[t, a, 2 + d], r2.at[t, a, 2 + d])
        sent(G.at[t, :, :, :, c], ssib.at[t], rsib.at[t])
        return carry

    def drain3(h, carry):
        for d in range(3):
            sent(lbuf.at[h, g], sl.at[h, d], rl.at[h, d])
            sent(tbuf.at[h, y], st.at[h, d], rt.at[h, d])
        for d in (0, 1):
            sent(gall.at[x, h], sx.at[h, d], rx.at[h, d])
            sent(half_rows(x, h, 0), sx.at[h, 2 + d], rx.at[h, 2 + d])
        return carry

    lax.fori_loop(0, pieces, drain1, 0)
    lax.fori_loop(0, steps, drain2, 0)
    lax.fori_loop(0, heads, drain3, 0)
    for q in range(4):
        @pl.when(jnp.logical_not(corner & (y == q)))
        def _():
            sent(out_unit(x, q), sa.at[q], ra.at[q])


def local(tokens, in_panels, out_panel, decay_power, boundary):
    slab_rows = tokens[0]
    extent, depth = slab_rows.shape
    seq_count = lax.axis_size("seq")
    own = lax.axis_index("seq")
    prompt_start = boundary[0]
    heads = decay_power.shape[0]
    rows = in_panels.shape[0]
    log_rate = log_half * jnp.exp2(decay_power.astype(F32)) / (extent * seq_count)

    shard = in_panels.reshape(rows, 2, 2, heads, HDIM).transpose(3, 1, 0, 2, 4)
    shard = shard.reshape(heads, 2, rows, 2 * HDIM)
    out_shard = out_panel.T

    crossing = prompt_start // extent

    def left(k, p):
        clear = (k < p) & ~((k < crossing) & (crossing < p))
        span = extent * jnp.maximum(p - 1 - k, 0).astype(F32)
        return jnp.where(clear[None], jnp.exp(log_rate[:, None] * span[None]), 0.0)

    four = jnp.arange(4, dtype=jnp.int32)
    base = own // 4 * 4
    coef = jnp.concatenate(
        [
            left(base + four, base + 4),
            left(base + four, own),
            left(4 * four + 3, own),
            jnp.exp(log_rate)[:, None],
            jnp.exp(log_rate * (extent - 1))[:, None],
            jnp.zeros((heads, 2), F32),
        ],
        axis=1,
    )
    place = (prompt_start - own * extent)[None]

    any_space = pl.BlockSpec(memory_space=pl.ANY)
    smem = pl.BlockSpec(memory_space=pltpu.SMEM)
    dma = pltpu.SemaphoreType.DMA
    steps = heads + 2
    columns = out_panel.shape[1] * 8
    result = pl.pallas_call(
        functools.partial(kernel, heads),
        out_shape=jax.ShapeDtypeStruct((extent, columns), BF16),
        in_specs=[smem, smem, smem, any_space, any_space, any_space],
        out_specs=pl.BlockSpec(memory_space=pltpu.VMEM),
        scratch_shapes=[
            pltpu.VMEM((steps, 2, 4, 2, 2, 2, rows, 2 * HDIM), BF16),
            pltpu.VMEM((extent, depth), BF16),
            pltpu.VMEM((4, heads, extent, HDIM), BF16),
            pltpu.VMEM((4, extent, HDIM), BF16),
            pltpu.VMEM((4, extent, HDIM), F32),
            pltpu.VMEM((4, extent, HDIM), F32),
            pltpu.VMEM((4, HDIM, HDIM), F32),
            pltpu.VMEM((heads, 4, HDIM, HDIM), BF16),
            pltpu.VMEM((heads, 4, HDIM, HDIM), BF16),
            pltpu.VMEM((extent, columns), F32),
            dma((3,)),
            dma((steps // 2, 2, 4)),
            dma((steps // 2, 2, 4)),
            dma((steps, 2, 4)),
            dma((steps, 2, 4)),
            dma((steps,)),
            dma((steps,)),
            dma((4,)),
            dma((4,)),
            dma((heads, 3)),
            dma((heads, 3)),
            dma((heads, 3)),
            dma((heads, 3)),
            dma((heads, 4)),
            dma((heads, 4)),
        ],
        compiler_params=pltpu.CompilerParams(
            collective_id=0, has_side_effects=True, vmem_limit_bytes=60 * 1024 * 1024
        ),
        cost_estimate=pl.CostEstimate(
            flops=2 * extent * depth * 4 * heads * HDIM, bytes_accessed=8_000_000, transcendentals=0
        ),
    )(log_rate, coef, place, slab_rows, shard, out_shard)
    return result[None]


def solution(mesh):
    return jax.shard_map(
        local,
        mesh=mesh,
        in_specs=(
            P("rep", "seq", None),
            P(("seq", "rep"), None, "tp"),
            P("tp", ("seq", "rep")),
            P("tp"),
            P("rep"),
        ),
        out_specs=P("rep", "seq", "tp"),
        check_vma=False,
    )
```

```python
import functools

import jax
import jax.numpy as jnp
from jax import lax
from jax.experimental import pallas as pl
from jax.experimental.pallas import tpu as pltpu
from jax.sharding import PartitionSpec as P

HDIM = 128
MESH = pl.DeviceIdType.MESH
log_half = -0.6931471805599453
epsilon = 1e-06
F32 = jnp.float32
BF16 = jnp.bfloat16


def nt_dot(a, b):
    return lax.dot_general(a, b, (((1,), (1,)), ((), ())), preferred_element_type=F32)


def tn_dot(a, b):
    return lax.dot_general(a, b, (((0,), (0,)), ((), ())), preferred_element_type=F32)


def kernel(
    heads, rates, coef, place, tok, wsh, osh, out,
    G, tokv, gall, qbuf, wbuf, gbuf, lout, lbuf, tbuf, eout, ebuf, acc, stage,
    loc, s1, r1, s2, r2, ssib, rsib, sa, ra, sl, rl, st, rt, se, re, sx, rx,
):
    extent = tok.shape[0]
    rows = wsh.shape[2]
    half = rows // 2
    steps = heads + 2
    rem, div = lax.rem, lax.div
    s, x, zhi = lax.axis_index("seq"), lax.axis_index("tp"), lax.axis_index("rep")
    y, g, zlo, c = div(s, 4), rem(s, 4), rem(div(s, 2), 2), rem(s, 2)
    z = zhi * 2 + zlo

    def around(k, d):
        return rem(k + d, 4)

    def at_y(k):
        return {"seq": k * 4 + g}

    def at_z(k):
        return {"seq": y * 4 + rem(k, 2) * 2 + c, "rep": div(k, 2)}

    def at_g(k):
        return {"seq": y * 4 + k}

    def at_x(k):
        return {"tp": k}

    sibling = {"seq": y * 4 + zlo * 2 + 1 - c}

    barrier = pltpu.get_barrier_semaphore()

    def greet(device):
        pl.semaphore_signal(barrier, inc=1, device_id=device, device_id_type=MESH)

    own_copies = [
        pltpu.make_async_copy(tok, tokv, loc.at[0]),
        pltpu.make_async_copy(wsh, G.at[pl.ds(0, heads), :, y, zlo, c, zhi], loc.at[1]),
        pltpu.make_async_copy(osh.at[y], stage.at[y], loc.at[2]),
    ]
    own_copies[1].start()
    own_copies[2].start()
    for d in (1, 2, 3):
        greet(at_y(around(y, d)))
        greet(at_g(around(g, d)))
        greet(at_x(around(x, d)))
    for d in (1, 3):
        greet(at_z(around(z, d)))
    pl.semaphore_wait(barrier, 11)

    def send(src, dst, ss, rs, device):
        pltpu.make_async_remote_copy(
            src_ref=src, dst_ref=dst, send_sem=ss, recv_sem=rs, device_id=device, device_id_type=MESH
        ).start()

    def got(ref, ss, rs):
        pltpu.make_async_remote_copy(
            src_ref=ref, dst_ref=ref, send_sem=ss, recv_sem=rs, device_id=sibling, device_id_type=MESH
        ).wait_recv()

    def sent(ref, ss, rs):
        pltpu.make_async_remote_copy(
            src_ref=ref, dst_ref=ref, send_sem=ss, recv_sem=rs, device_id=sibling, device_id_type=MESH
        ).wait_send()

    first_ring = ((y, at_y), (z, at_z))
    second_ring = ((z, at_z), (y, at_y))

    def unit1(m, a, k, lo=0, n=rows):
        if a == 0:
            return G.at[m, 0, k, zlo, c, zhi, pl.ds(lo, n)]
        return G.at[m, 1, y, rem(k, 2), c, div(k, 2), pl.ds(lo, n)]

    def unit2(t, a, k):
        if a == 0:
            return G.at[t, 0, :, rem(k, 2), c, div(k, 2)]
        return G.at[t, 1, k, :, c]

    def half2(t, a, k, part):
        if a == 0:
            return G.at[t, 0, pl.ds(2 * part, 2), rem(k, 2), c, div(k, 2)]
        return G.at[t, 1, k, pl.ds(part, 1), c]

    SLOTS = 4

    def slot_of(m):
        return rem(m, SLOTS)

    def reused(m, wait):
        if isinstance(m, int):
            if m >= SLOTS:
                wait()
        else:
            pl.when(m >= SLOTS)(wait)

    def first_sent(k):
        sent(G.at[0, 0, pl.ds(0, 3), :, 0, 0], s1.at[k], s1.at[k])

    def second_sent(k):
        sent(G.at[0, 0, pl.ds(0, 3)], s2.at[k], s2.at[k])

    def first_send(m):
        k0 = slot_of(m)
        reused(m, lambda: first_sent(k0))
        for a in (0, 1):
            k, at = first_ring[a]
            own = unit1(m, a, k)
            for d, step in ((0, 1), (1, 3)):
                send(own, own, s1.at[k0], r1.at[k0, a, d], at(around(k, step)))

    def first_pass(m):
        k0 = slot_of(m)
        for a in (0, 1):
            k, at = first_ring[a]
            for d, step in ((0, 1), (1, 3)):
                origin = around(k, 4 - step)
                got(unit1(m, a, origin), s1.at[k0], r1.at[k0, a, d])
                part = unit1(m, a, origin, d * half, half)
                send(part, part, s1.at[k0], r1.at[k0, a, 2], at(around(k, step)))

    def first_end(m):
        k0 = slot_of(m)
        for a in (0, 1):
            k, _ = first_ring[a]
            got(unit1(m, a, around(k, 2)), s1.at[k0], r1.at[k0, a, 2])

    def second_send(t):
        k0 = slot_of(t)
        reused(t, lambda: second_sent(k0))
        for a in (1, 0):
            k, at = second_ring[a]
            own = unit2(t, a, k)
            for d, step in ((0, 1), (1, 3)):
                send(own, own, s2.at[k0], r2.at[k0, a, d], at(around(k, step)))

    def second_pass(t):
        k0 = slot_of(t)
        for a in (1, 0):
            k, at = second_ring[a]
            for d, step in ((0, 1), (1, 3)):
                origin = around(k, 4 - step)
                got(unit2(t, a, origin), s2.at[k0], r2.at[k0, a, d])
                part = half2(t, a, origin, d)
                send(part, part, s2.at[k0], r2.at[k0, a, 2], at(around(k, step)))

    def second_end(t):
        k0 = slot_of(t)
        for a in (1, 0):
            k, _ = second_ring[a]
            got(unit2(t, a, around(k, 2)), s2.at[k0], r2.at[k0, a, 2])

    def share_sent(k):
        sent(G.at[0, :, :, :, c], ssib.at[k], ssib.at[k])

    def share(t):
        k0 = slot_of(t)
        reused(t, lambda: share_sent(k0))
        mine = G.at[t, :, :, :, c]
        send(mine, mine, ssib.at[k0], rsib.at[k0], sibling)

    def shared(t):
        k0 = slot_of(t)
        got(G.at[t, :, :, :, 1 - c], ssib.at[k0], rsib.at[k0])

    def out_unit(k, q):
        return G.at[heads + div(k, 2), rem(k, 2), q, zlo, c, zhi]

    def regroup_y():
        for d in (1, 2, 3):
            q = around(y, d)
            send(osh.at[q], stage.at[y], sa.at[0], ra.at[0], at_y(q))

    def regroup_x():
        own_copies[2].wait()
        got(stage.at[pl.ds(0, 3)], sa.at[0], ra.at[0])
        pltpu.make_async_copy(stage.at[x], out_unit(x, y), loc.at[2]).start()
        for d in (1, 2, 3):
            k = around(x, d)
            send(stage.at[k], out_unit(x, y), sa.at[1], ra.at[1], at_x(k))

    def regrouped():
        pltpu.make_async_copy(stage.at[x], out_unit(x, y), loc.at[2]).wait()
        got(stage.at[pl.ds(0, 3)], sa.at[1], ra.at[1])

    own_copies[1].wait()
    first_send(0)
    first_send(1)
    regroup_y()
    own_copies[0].start()
    first_pass(0)
    first_send(2)
    first_pass(1)
    first_end(0)
    second_send(0)
    first_pass(2)
    first_send(3)
    regroup_x()
    acc[...] = jnp.zeros_like(acc)
    own_copies[0].wait()

    edge = place[0]
    down = lax.broadcasted_iota(jnp.int32, (extent, HDIM), 0)
    BR = 256
    QR = HDIM // 4

    def blocks_sent(sem):
        sent(lbuf.at[0, pl.ds(0, 3)], sem, sem)

    def gated_sent(k):
        sent(gall.at[pl.ds(0, 3), 0], sx.at[k], sx.at[k])

    def project(h):
        slot = rem(h, 4)
        rate = rates[h]
        panel = G[h, 0].reshape(-1, 2 * HDIM)
        u = jnp.dot(tokv[...], panel, preferred_element_type=F32)
        down_f = down.astype(F32)
        grow = jnp.exp(rate * down_f)
        shrink = jnp.exp(-rate * down_f)
        uq, uk = u[:, :HDIM], u[:, HDIM:]
        q = ((uq / (1.0 + jnp.exp(-uq))) * (HDIM ** -0.5) * grow).astype(BF16)
        kf = (uk / (1.0 + jnp.exp(-uk))) * shrink
        k = kf.astype(BF16)
        kept = jnp.where((down >= edge) | (edge >= extent), kf, 0.0).astype(BF16)
        panel = G[h, 1].reshape(-1, 2 * HDIM)
        u = jnp.dot(tokv[...], panel, preferred_element_type=F32)
        v = u[:, :HDIM].astype(BF16)
        gbuf[slot] = 1.0 / (1.0 + jnp.exp(-u[:, HDIM:]))
        qbuf[slot] = q
        k0 = slot_of(h)
        reused(h, lambda: blocks_sent(sl.at[k0]))
        added = (tn_dot(kept, v) * coef[h, 37]).astype(BF16)
        lout[k0] = added
        lbuf[h, g] = lout[k0, pl.ds(g * QR, QR)]
        for d in (1, 2, 3):
            to = around(g, d)
            send(lout.at[k0, pl.ds(to * QR, QR)], lbuf.at[h, g], sl.at[k0], rl.at[k0], at_g(to))
        for lo in range(0, extent, BR):
            hi = lo + BR
            scores = nt_dot(q[lo:hi], k[:hi])
            i = lax.broadcasted_iota(jnp.int32, (BR, hi), 0) + lo
            j = lax.broadcasted_iota(jnp.int32, (BR, hi), 1)
            keep = (j <= i) & (j >= jnp.where(i >= edge, edge, 0))
            scores = jnp.where(keep, scores, 0.0).astype(BF16)
            wbuf[slot, pl.ds(lo, BR)] = jnp.dot(scores, v[:hi], preferred_element_type=F32)

    def gather_states(h):
        k0 = slot_of(h)
        got(lbuf.at[h, pl.ds(0, 3)], sl.at[k0], rl.at[k0])
        total = coef[h, 0] * lbuf[h, 0].astype(F32)
        for k in range(1, 4):
            total += coef[h, k] * lbuf[h, k].astype(F32)
        reused(h, lambda: blocks_sent(st.at[k0]))
        tbuf[h, y] = total.astype(BF16)
        for d in (1, 2, 3):
            own = tbuf.at[h, y]
            send(own, own, st.at[k0], rt.at[k0], at_y(around(y, d)))

    def spread_states(h):
        k0 = slot_of(h)
        got(tbuf.at[h, pl.ds(0, 3)], st.at[k0], rt.at[k0])
        reused(h, lambda: blocks_sent(se.at[k0]))
        for p in range(4):
            state = jnp.zeros((QR, HDIM), F32)
            for k in range(4):
                state += coef[h, 4 + 8 * p + k] * lbuf[h, k].astype(F32)
                state += coef[h, 8 + 8 * p + k] * tbuf[h, k].astype(F32)
            eout[k0, p] = state.astype(BF16)
        ebuf[h, g] = eout[k0, g]
        for d in (1, 2, 3):
            k = around(g, d)
            send(eout.at[k0, k], ebuf.at[h, g], se.at[k0], re.at[k0], at_g(k))

    def finish(h):
        slot = rem(h, 4)
        k0 = slot_of(h)
        got(ebuf.at[h, pl.ds(0, 3)], se.at[k0], re.at[k0])
        state = ebuf[h].reshape(HDIM, HDIM)
        use = jnp.where((down < edge) | (edge < 0), coef[h, 36], 0.0)
        across = jnp.dot(qbuf[slot], state, preferred_element_type=F32)
        attended = wbuf[slot] + across * use
        square = jnp.mean(attended * attended, axis=-1, keepdims=True)
        gall[x, h] = (attended * lax.rsqrt(square + epsilon) * gbuf[slot]).astype(BF16)
        reused(h, lambda: gated_sent(k0))
        own = gall.at[x, h]
        for d, step in ((0, 1), (1, 3)):
            send(own, own, sx.at[k0], rx.at[k0, d], at_x(around(x, step)))

    def half_rows(k, h, d):
        return gall.at[k, h, pl.ds(d * (extent // 2), extent // 2)]

    def pass_gated(h):
        k0 = slot_of(h)
        for d, step in ((0, 1), (1, 3)):
            origin = around(x, 4 - step)
            got(gall.at[origin, h], sx.at[k0], rx.at[k0, d])
            part = half_rows(origin, h, d)
            send(part, part, sx.at[k0], rx.at[k0, 2], at_x(around(x, step)))

    def end_gated(h):
        k0 = slot_of(h)
        got(gall.at[around(x, 2), h], sx.at[k0], rx.at[k0, 2])

    def emit(i, q):
        panel = jnp.concatenate(
            [G[heads + i, a, q].reshape(-1, 2 * HDIM) for a in (0, 1)], axis=1
        )
        for lo in range(0, extent, BR):
            left = jnp.concatenate(
                [gall[2 * i + a, 2 * q + b, pl.ds(lo, BR)] for a in (0, 1) for b in (0, 1)], axis=1
            )
            acc[pl.ds(lo, BR)] += nt_dot(left, panel)

    def turn(n, carry):
        t = n - 1

        def when(lag, count):
            return pl.when((t >= lag) & (t - lag < count))

        @when(-1, steps)
        def _():
            second_pass(t + 1)
        @when(2, heads)
        def _():
            finish(t - 2)
        @when(1, heads)
        def _():
            gather_states(t - 1)
        @pl.when(t + 2 < steps)
        def _():
            first_end(t + 2)
            second_send(t + 2)
        @pl.when(t + 4 < steps)
        def _():
            first_pass(t + 4)
        @pl.when(t + 5 == heads)
        def _():
            regrouped()
        @pl.when(t + 5 < steps)
        def _():
            first_send(t + 5)
        @when(0, steps)
        def _():
            shared(t)
        @when(0, heads)
        def _():
            project(t)
        @when(1, heads)
        def _():
            spread_states(t - 1)
        @when(2, heads)
        def _():
            pass_gated(t - 2)
        @when(-1, steps)
        def _():
            second_end(t + 1)
            share(t + 1)
        @when(3, heads)
        def _():
            end_gated(t - 3)
        @when(heads, 2)
        def _():
            def add(q, carry):
                emit(t - heads, q)
                return carry
            lax.fori_loop(0, 2, add, 0)
        return carry

    lax.fori_loop(0, steps + 1, turn, 0)

    def both(q):
        lax.fori_loop(0, 2, lambda i, carry: (emit(i, q), carry)[1], 0)

    both(2)
    end_gated(heads - 1)
    both(3)
    out[...] = acc[...].astype(out.dtype)

    for k in range(SLOTS):
        first_sent(k)
        second_sent(k)
        share_sent(k)
        blocks_sent(sl.at[k])
        blocks_sent(st.at[k])
        blocks_sent(se.at[k])
        gated_sent(k)
    for k in range(2):
        sent(stage.at[pl.ds(0, 3)], sa.at[k], sa.at[k])


def local(tokens, in_panels, out_panel, decay_power, boundary):
    slab_rows = tokens[0]
    extent, depth = slab_rows.shape
    seq_count = lax.axis_size("seq")
    own = lax.axis_index("seq")
    prompt_start = boundary[0]
    heads = decay_power.shape[0]
    rows = in_panels.shape[0]
    log_rate = log_half * jnp.exp2(decay_power.astype(F32)) / (extent * seq_count)

    shard = in_panels.reshape(rows, 2, 2, heads, HDIM).transpose(3, 1, 0, 2, 4)
    shard = shard.reshape(heads, 2, rows, 2 * HDIM)
    out_shard = out_panel.T.reshape(rows, 4, -1).transpose(1, 0, 2)

    crossing = prompt_start // extent

    def left(k, p):
        clear = (k < p) & ~((k < crossing) & (crossing < p))
        span = extent * jnp.maximum(p - 1 - k, 0).astype(F32)
        return jnp.where(clear[None], jnp.exp(log_rate[:, None] * span[None]), 0.0)

    four = jnp.arange(4, dtype=jnp.int32)
    base = own // 4 * 4
    coef = jnp.concatenate(
        [
            left(base + four, base + 4),
            *[
                left(origin, base + k)
                for k in range(4)
                for origin in (base + four, 4 * four + 3)
            ],
            jnp.exp(log_rate)[:, None],
            jnp.exp(log_rate * (extent - 1))[:, None],
        ],
        axis=1,
    )
    place = (prompt_start - own * extent)[None]

    any_space = pl.BlockSpec(memory_space=pl.ANY)
    smem = pl.BlockSpec(memory_space=pltpu.SMEM)
    dma = pltpu.SemaphoreType.DMA
    steps = heads + 2
    columns = out_panel.shape[1] * 8
    result = pl.pallas_call(
        functools.partial(kernel, heads),
        out_shape=jax.ShapeDtypeStruct((extent, columns), BF16),
        in_specs=[smem, smem, smem, any_space, any_space, any_space],
        out_specs=pl.BlockSpec(memory_space=pltpu.VMEM),
        scratch_shapes=[
            pltpu.VMEM((steps, 2, 4, 2, 2, 2, rows, 2 * HDIM), BF16),
            pltpu.VMEM((extent, depth), BF16),
            pltpu.VMEM((4, heads, extent, HDIM), BF16),
            pltpu.VMEM((4, extent, HDIM), BF16),
            pltpu.VMEM((4, extent, HDIM), F32),
            pltpu.VMEM((4, extent, HDIM), F32),
            pltpu.VMEM((4, HDIM, HDIM), BF16),
            pltpu.VMEM((heads, 4, HDIM // 4, HDIM), BF16),
            pltpu.VMEM((heads, 4, HDIM // 4, HDIM), BF16),
            pltpu.VMEM((4, 4, HDIM // 4, HDIM), BF16),
            pltpu.VMEM((heads, 4, HDIM // 4, HDIM), BF16),
            pltpu.VMEM((extent, columns), F32),
            pltpu.VMEM((4, out_panel.shape[1], out_panel.shape[0] // 4), BF16),
            dma((3,)),
            dma((4,)),
            dma((4, 2, 3)),
            dma((4,)),
            dma((4, 2, 3)),
            dma((4,)),
            dma((4,)),
            dma((2,)),
            dma((2,)),
            dma((4,)),
            dma((4,)),
            dma((4,)),
            dma((4,)),
            dma((4,)),
            dma((4,)),
            dma((4,)),
            dma((4, 3)),
        ],
        compiler_params=pltpu.CompilerParams(
            collective_id=0, has_side_effects=True, vmem_limit_bytes=60 * 1024 * 1024
        ),
        cost_estimate=pl.CostEstimate(
            flops=2 * extent * depth * 4 * heads * HDIM, bytes_accessed=8_000_000, transcendentals=0
        ),
    )(log_rate, coef, place, slab_rows, shard, out_shard)
    return result[None]


def solution(mesh):
    return jax.shard_map(
        local,
        mesh=mesh,
        in_specs=(
            P("rep", "seq", None),
            P(("seq", "rep"), None, "tp"),
            P("tp", ("seq", "rep")),
            P("tp"),
            P("rep"),
        ),
        out_specs=P("rep", "seq", "tp"),
        check_vma=False,
    )
```

```python
import functools

import jax
import jax.numpy as jnp
from jax import lax
from jax.experimental import pallas as pl
from jax.experimental.pallas import tpu as pltpu
from jax.sharding import PartitionSpec as P

HDIM = 128
MESH = pl.DeviceIdType.MESH
log_half = -0.6931471805599453
epsilon = 1e-06
F32 = jnp.float32
BF16 = jnp.bfloat16


def nt_dot(a, b):
    return lax.dot_general(a, b, (((1,), (1,)), ((), ())), preferred_element_type=F32)


def tn_dot(a, b):
    return lax.dot_general(a, b, (((0,), (0,)), ((), ())), preferred_element_type=F32)


def kernel(
    heads, blocks, powers, place, tok, wsh, osh, out,
    G, tokv, gall, qbuf, wbuf, gbuf, lout, lbuf, tbuf, eout, ebuf, acc, stage,
    loc, s1, r1, s2, r2, ssib, rsib, sa, ra, sl, rl, st, rt, se, re, sx, rx,
):
    extent = tok.shape[0]
    rows = wsh.shape[2]
    half = rows // 2
    steps = heads + 2
    rem, div = lax.rem, lax.div
    s, x, zhi = lax.axis_index("seq"), lax.axis_index("tp"), lax.axis_index("rep")
    y, g, zlo, c = div(s, 4), rem(s, 4), rem(div(s, 2), 2), rem(s, 2)
    z = zhi * 2 + zlo

    def around(k, d):
        return rem(k + d, 4)

    def at_y(k):
        return {"seq": k * 4 + g}

    def at_z(k):
        return {"seq": y * 4 + rem(k, 2) * 2 + c, "rep": div(k, 2)}

    def at_g(k):
        return {"seq": y * 4 + k}

    def at_x(k):
        return {"tp": k}

    sibling = {"seq": y * 4 + zlo * 2 + 1 - c}

    barrier = pltpu.get_barrier_semaphore()

    def greet(device):
        pl.semaphore_signal(barrier, inc=1, device_id=device, device_id_type=MESH)

    def quarter(q):
        width = osh.shape[1] // 4
        return osh.at[:, pl.ds(pl.multiple_of(q * width, width), width)]

    own_copies = [
        pltpu.make_async_copy(tok, tokv, loc.at[0]),
        pltpu.make_async_copy(wsh, G.at[pl.ds(0, heads), :, y, zlo, c, zhi], loc.at[1]),
        pltpu.make_async_copy(quarter(y), stage.at[y], loc.at[2]),
    ]
    own_copies[1].start()
    own_copies[2].start()
    for d in (1, 2, 3):
        greet(at_y(around(y, d)))
        greet(at_g(around(g, d)))
        greet(at_x(around(x, d)))
    for d in (1, 3):
        greet(at_z(around(z, d)))
    pl.semaphore_wait(barrier, 11)

    def send(src, dst, ss, rs, device):
        pltpu.make_async_remote_copy(
            src_ref=src, dst_ref=dst, send_sem=ss, recv_sem=rs, device_id=device, device_id_type=MESH
        ).start()

    def got(ref, ss, rs):
        pltpu.make_async_remote_copy(
            src_ref=ref, dst_ref=ref, send_sem=ss, recv_sem=rs, device_id=sibling, device_id_type=MESH
        ).wait_recv()

    def sent(ref, ss, rs):
        pltpu.make_async_remote_copy(
            src_ref=ref, dst_ref=ref, send_sem=ss, recv_sem=rs, device_id=sibling, device_id_type=MESH
        ).wait_send()

    first_ring = ((y, at_y), (z, at_z))
    second_ring = ((z, at_z), (y, at_y))

    def unit1(m, a, k, lo=0, n=rows):
        if a == 0:
            return G.at[m, 0, k, zlo, c, zhi, pl.ds(lo, n)]
        return G.at[m, 1, y, rem(k, 2), c, div(k, 2), pl.ds(lo, n)]

    def unit2(t, a, k):
        if a == 0:
            return G.at[t, 0, :, rem(k, 2), c, div(k, 2)]
        return G.at[t, 1, k, :, c]

    def half2(t, a, k, part):
        if a == 0:
            return G.at[t, 0, pl.ds(2 * part, 2), rem(k, 2), c, div(k, 2)]
        return G.at[t, 1, k, pl.ds(part, 1), c]

    SLOTS = 4

    def slot_of(m):
        return rem(m, SLOTS)

    def reused(m, wait):
        if isinstance(m, int):
            if m >= SLOTS:
                wait()
        else:
            pl.when(m >= SLOTS)(wait)

    def first_sent(k):
        sent(G.at[0, 0, pl.ds(0, 3), :, 0, 0], s1.at[k], s1.at[k])

    def second_sent(k):
        sent(G.at[0, 0, pl.ds(0, 3)], s2.at[k], s2.at[k])

    def first_send(m):
        k0 = slot_of(m)
        reused(m, lambda: first_sent(k0))
        for a in (0, 1):
            k, at = first_ring[a]
            own = unit1(m, a, k)
            start = wsh.at[m, a] if isinstance(m, int) else own
            for d, step in ((0, 1), (1, 3)):
                send(start, own, s1.at[k0], r1.at[k0, a, d], at(around(k, step)))

    def first_pass(m):
        k0 = slot_of(m)
        for a in (0, 1):
            k, at = first_ring[a]
            for d, step in ((0, 1), (1, 3)):
                origin = around(k, 4 - step)
                got(unit1(m, a, origin), s1.at[k0], r1.at[k0, a, d])
                part = unit1(m, a, origin, d * half, half)
                send(part, part, s1.at[k0], r1.at[k0, a, 2], at(around(k, step)))

    def first_end(m):
        k0 = slot_of(m)
        for a in (0, 1):
            k, _ = first_ring[a]
            got(unit1(m, a, around(k, 2)), s1.at[k0], r1.at[k0, a, 2])

    def second_send_one(t, a, d):
        k0 = slot_of(t)
        k, at = second_ring[a]
        for n in (0, 1):
            own = half2(t, a, k, (d + n) % 2)
            send(own, own, s2.at[k0], r2.at[k0, a, d + 3 * n], at(around(k, 3 if d else 1)))

    def second_pass_one(t, a, d):
        k0 = slot_of(t)
        k, at = second_ring[a]
        step = 3 if d else 1
        origin = around(k, 4 - step)
        part = half2(t, a, origin, d)
        got(part, s2.at[k0], r2.at[k0, a, d])
        send(part, part, s2.at[k0], r2.at[k0, a, 2], at(around(k, step)))

    def second_end(t):
        k0 = slot_of(t)
        for a in (1, 0):
            k, _ = second_ring[a]
            for d in (0, 1):
                got(half2(t, a, k, d), s2.at[k0], r2.at[k0, a, 3 + d])
            got(unit2(t, a, around(k, 2)), s2.at[k0], r2.at[k0, a, 2])

    def share_sent(k):
        sent(G.at[0, :, :, :, c], ssib.at[k], ssib.at[k])

    def share(t):
        k0 = slot_of(t)
        reused(t, lambda: share_sent(k0))
        mine = G.at[t, :, :, :, c]
        send(mine, mine, ssib.at[k0], rsib.at[k0], sibling)

    def shared(t):
        k0 = slot_of(t)
        got(G.at[t, :, :, :, 1 - c], ssib.at[k0], rsib.at[k0])

    def out_unit(k, q):
        return G.at[heads + div(k, 2), rem(k, 2), q, zlo, c, zhi]

    def regroup_y():
        for d in (1, 2, 3):
            q = around(y, d)
            send(quarter(q), stage.at[y], sa.at[0], ra.at[0], at_y(q))

    def regroup_x():
        own_copies[2].wait()
        got(stage.at[pl.ds(0, 3)], sa.at[0], ra.at[0])
        pltpu.make_async_copy(stage.at[x], out_unit(x, y), loc.at[2]).start()
        for d in (1, 2, 3):
            k = around(x, d)
            send(stage.at[k], out_unit(x, y), sa.at[1], ra.at[1], at_x(k))

    def regrouped():
        pltpu.make_async_copy(stage.at[x], out_unit(x, y), loc.at[2]).wait()
        got(stage.at[pl.ds(0, 3)], sa.at[1], ra.at[1])

    first_send(0)
    first_send(1)
    first_send(2)
    regroup_y()
    own_copies[0].start()
    first_pass(0)
    own_copies[1].wait()
    first_pass(1)
    first_end(0)
    for a in (0, 1):
        for d in (0, 1):
            second_send_one(0, a, d)
    first_pass(2)
    first_send(3)
    regroup_x()
    acc[...] = jnp.zeros_like(acc)
    own_copies[0].wait()

    edge = place[0] - s * extent
    crossing = div(place[0], extent)
    base = y * 4

    def rate_of(h):
        return (log_half / (extent * blocks)) * jnp.left_shift(1, powers[h]).astype(F32)

    def left(h, k, p):
        clear = (k < p) & jnp.logical_not((k < crossing) & (crossing < p))
        span = (extent * jnp.maximum(p - 1 - k, 0)).astype(F32)
        share = jnp.exp(jnp.full((8, HDIM), rate_of(h) * span, F32))[:1]
        return jnp.where(clear, share, 0.0)

    down = lax.broadcasted_iota(jnp.int32, (extent, HDIM), 0)
    BR = 256
    QR = HDIM // 4

    def blocks_sent(sem):
        sent(lbuf.at[0, pl.ds(0, 3)], sem, sem)

    def gated_sent(k):
        sent(gall.at[pl.ds(0, 3), 0], sx.at[k], sx.at[k])

    def project(h):
        slot = rem(h, 4)
        rate = rate_of(h)
        panel = G[h, 0].reshape(-1, 2 * HDIM)
        u = jnp.dot(tokv[...], panel, preferred_element_type=F32)
        down_f = down.astype(F32)
        grow = jnp.exp(rate * down_f)
        shrink = jnp.exp(-rate * down_f)
        uq, uk = u[:, :HDIM], u[:, HDIM:]
        q = ((uq / (1.0 + jnp.exp(-uq))) * (HDIM ** -0.5) * grow).astype(BF16)
        kf = (uk / (1.0 + jnp.exp(-uk))) * shrink
        k = kf.astype(BF16)
        kept = jnp.where((down >= edge) | (edge >= extent), kf, 0.0).astype(BF16)
        panel = G[h, 1].reshape(-1, 2 * HDIM)
        u = jnp.dot(tokv[...], panel, preferred_element_type=F32)
        v = u[:, :HDIM].astype(BF16)
        gbuf[slot] = 1.0 / (1.0 + jnp.exp(-u[:, HDIM:]))
        qbuf[slot] = q
        k0 = slot_of(h)
        reused(h, lambda: blocks_sent(sl.at[k0]))
        added = (tn_dot(kept, v) * jnp.exp(jnp.full((8, HDIM), rate * (extent - 1), F32))[:1]).astype(BF16)
        lout[k0] = added
        lbuf[h, g] = lout[k0, pl.ds(g * QR, QR)]
        for d in (1, 2, 3):
            to = around(g, d)
            send(lout.at[k0, pl.ds(to * QR, QR)], lbuf.at[h, g], sl.at[k0], rl.at[k0], at_g(to))
        for lo in range(0, extent, BR):
            hi = lo + BR
            scores = nt_dot(q[lo:hi], k[:hi])
            i = lax.broadcasted_iota(jnp.int32, (BR, hi), 0) + lo
            j = lax.broadcasted_iota(jnp.int32, (BR, hi), 1)
            keep = (j <= i) & (j >= jnp.where(i >= edge, edge, 0))
            scores = jnp.where(keep, scores, 0.0).astype(BF16)
            wbuf[slot, pl.ds(lo, BR)] = jnp.dot(scores, v[:hi], preferred_element_type=F32)

    def gather_states(h):
        k0 = slot_of(h)
        got(lbuf.at[h, pl.ds(0, 3)], sl.at[k0], rl.at[k0])
        total = jnp.zeros((QR, HDIM), F32)
        for k in range(4):
            total += left(h, base + k, base + 4) * lbuf[h, k].astype(F32)
        reused(h, lambda: blocks_sent(st.at[k0]))
        tbuf[h, y] = total.astype(BF16)
        for d in (1, 2, 3):
            own = tbuf.at[h, y]
            send(own, own, st.at[k0], rt.at[k0], at_y(around(y, d)))

    def spread_states(h):
        k0 = slot_of(h)
        got(tbuf.at[h, pl.ds(0, 3)], st.at[k0], rt.at[k0])
        reused(h, lambda: blocks_sent(se.at[k0]))
        for p in range(4):
            state = jnp.zeros((QR, HDIM), F32)
            for k in range(4):
                if k < p:
                    state += left(h, base + k, base + p) * lbuf[h, k].astype(F32)
                state += left(h, 4 * k + 3, base + p) * tbuf[h, k].astype(F32)
            eout[k0, p] = state.astype(BF16)
        ebuf[h, g] = eout[k0, g]
        for d in (1, 2, 3):
            k = around(g, d)
            send(eout.at[k0, k], ebuf.at[h, g], se.at[k0], re.at[k0], at_g(k))

    def finish(h):
        slot = rem(h, 4)
        k0 = slot_of(h)
        got(ebuf.at[h, pl.ds(0, 3)], se.at[k0], re.at[k0])
        state = ebuf[h].reshape(HDIM, HDIM)
        once = jnp.exp(jnp.full((8, HDIM), rate_of(h), F32))[:1]
        use = jnp.where((down < edge) | (edge < 0), once, 0.0)
        across = jnp.dot(qbuf[slot], state, preferred_element_type=F32)
        attended = wbuf[slot] + across * use
        square = jnp.mean(attended * attended, axis=-1, keepdims=True)
        gall[x, h] = (attended * lax.rsqrt(square + epsilon) * gbuf[slot]).astype(BF16)
        reused(h, lambda: gated_sent(k0))
        for n in (0, 1):
            for d, step in ((0, 1), (1, 3)):
                own = half_rows(x, h, (d + n) % 2)
                send(own, own, sx.at[k0], rx.at[k0, d + 3 * n], at_x(around(x, step)))

    def half_rows(k, h, d):
        return gall.at[k, h, pl.ds(d * (extent // 2), extent // 2)]

    def pass_gated(h):
        k0 = slot_of(h)
        for d, step in ((0, 1), (1, 3)):
            origin = around(x, 4 - step)
            part = half_rows(origin, h, d)
            got(part, sx.at[k0], rx.at[k0, d])
            send(part, part, sx.at[k0], rx.at[k0, 2], at_x(around(x, step)))

    def end_gated(h):
        k0 = slot_of(h)
        for d in (0, 1):
            got(half_rows(x, h, d), sx.at[k0], rx.at[k0, 3 + d])
        got(gall.at[around(x, 2), h], sx.at[k0], rx.at[k0, 2])

    def emit(i, q):
        panel = jnp.concatenate(
            [G[heads + i, a, q].reshape(-1, 2 * HDIM) for a in (0, 1)], axis=1
        )
        for lo in range(0, extent, BR):
            left = jnp.concatenate(
                [gall[2 * i + a, 2 * q + b, pl.ds(lo, BR)] for a in (0, 1) for b in (0, 1)], axis=1
            )
            acc[pl.ds(lo, BR)] += nt_dot(left, panel)

    def turn(n, carry):
        t = n - 1

        def when(lag, count):
            return pl.when((t >= lag) & (t - lag < count))

        @pl.when(t + 2 < steps)
        def _():
            first_end(t + 2)
            reused(t + 2, lambda: second_sent(slot_of(t + 2)))

        def ring(a, d):
            @when(-1, steps)
            def _():
                second_pass_one(t + 1, a, d)

        def own(a, d):
            @pl.when(t + 2 < steps)
            def _():
                second_send_one(t + 2, a, d)

        for d in (0, 1):
            ring(0, d)
            own(0, d)
        ring(1, 0)
        ring(1, 1)
        @when(1, heads)
        def _():
            gather_states(t - 1)
        own(1, 0)
        own(1, 1)
        @when(2, heads)
        def _():
            finish(t - 2)
        @when(0, steps)
        def _():
            shared(t)
        @when(0, heads)
        def _():
            project(t)
        @when(-1, steps)
        def _():
            second_end(t + 1)
        @when(-1, steps)
        def _():
            share(t + 1)
        @pl.when(t + 4 < steps)
        def _():
            first_pass(t + 4)
        @pl.when(t + 5 == heads)
        def _():
            regrouped()
        @pl.when(t + 5 < steps)
        def _():
            first_send(t + 5)
        @when(1, heads)
        def _():
            spread_states(t - 1)
        @pl.when(t == heads + 1)
        def _():
            lax.fori_loop(0, 4, lambda n, carry: (emit(div(n, 2), rem(n, 2)), carry)[1], 0)
        @when(2, heads)
        def _():
            pass_gated(t - 2)
        @when(3, heads)
        def _():
            end_gated(t - 3)
        return carry

    lax.fori_loop(0, steps + 1, turn, 0)

    def both(q):
        lax.fori_loop(0, 2, lambda i, carry: (emit(i, q), carry)[1], 0)

    both(2)
    end_gated(heads - 1)
    both(3)
    out[...] = acc[...].astype(out.dtype)

    for k in range(SLOTS):
        first_sent(k)
        second_sent(k)
        share_sent(k)
        blocks_sent(sl.at[k])
        blocks_sent(st.at[k])
        blocks_sent(se.at[k])
        gated_sent(k)
    for k in range(2):
        sent(stage.at[pl.ds(0, 3)], sa.at[k], sa.at[k])


def local(tokens, in_panels, out_panel, decay_power, boundary):
    slab_rows = tokens[0]
    extent, depth = slab_rows.shape
    seq_count = lax.axis_size("seq")
    heads = decay_power.shape[0]
    rows = in_panels.shape[0]
    shard = in_panels.reshape(rows, 2, 2, heads, HDIM).transpose(3, 1, 0, 2, 4)
    shard = shard.reshape(heads, 2, rows, 2 * HDIM)
    out_shard = out_panel.T

    any_space = pl.BlockSpec(memory_space=pl.ANY)
    smem = pl.BlockSpec(memory_space=pltpu.SMEM)
    dma = pltpu.SemaphoreType.DMA
    steps = heads + 2
    columns = out_panel.shape[1] * 8
    result = pl.pallas_call(
        functools.partial(kernel, heads, seq_count),
        out_shape=jax.ShapeDtypeStruct((extent, columns), BF16),
        in_specs=[smem, smem, any_space, any_space, any_space],
        out_specs=pl.BlockSpec(memory_space=pltpu.VMEM),
        scratch_shapes=[
            pltpu.VMEM((steps, 2, 4, 2, 2, 2, rows, 2 * HDIM), BF16),
            pltpu.VMEM((extent, depth), BF16),
            pltpu.VMEM((4, heads, extent, HDIM), BF16),
            pltpu.VMEM((4, extent, HDIM), BF16),
            pltpu.VMEM((4, extent, HDIM), F32),
            pltpu.VMEM((4, extent, HDIM), F32),
            pltpu.VMEM((4, HDIM, HDIM), BF16),
            pltpu.VMEM((heads, 4, HDIM // 4, HDIM), BF16),
            pltpu.VMEM((heads, 4, HDIM // 4, HDIM), BF16),
            pltpu.VMEM((4, 4, HDIM // 4, HDIM), BF16),
            pltpu.VMEM((heads, 4, HDIM // 4, HDIM), BF16),
            pltpu.VMEM((extent, columns), F32),
            pltpu.VMEM((4, out_panel.shape[1], out_panel.shape[0] // 4), BF16),
            dma((3,)),
            dma((4,)),
            dma((4, 2, 3)),
            dma((4,)),
            dma((4, 2, 5)),
            dma((4,)),
            dma((4,)),
            dma((2,)),
            dma((2,)),
            dma((4,)),
            dma((4,)),
            dma((4,)),
            dma((4,)),
            dma((4,)),
            dma((4,)),
            dma((4,)),
            dma((4, 5)),
        ],
        compiler_params=pltpu.CompilerParams(
            collective_id=0, has_side_effects=True, vmem_limit_bytes=60 * 1024 * 1024
        ),
        cost_estimate=pl.CostEstimate(
            flops=2 * extent * depth * 4 * heads * HDIM, bytes_accessed=8_000_000, transcendentals=0
        ),
    )(decay_power, boundary, slab_rows, shard, out_shard)
    return result[None]


def solution(mesh):
    return jax.shard_map(
        local,
        mesh=mesh,
        in_specs=(
            P("rep", "seq", None),
            P(("seq", "rep"), None, "tp"),
            P("tp", ("seq", "rep")),
            P("tp"),
            P("rep"),
        ),
        out_specs=P("rep", "seq", "tp"),
        check_vma=False,
    )
```

```python
import functools

import jax
import jax.numpy as jnp
from jax import lax
from jax.experimental import pallas as pl
from jax.experimental.pallas import tpu as pltpu
from jax.sharding import PartitionSpec as P

HDIM = 128
MESH = pl.DeviceIdType.MESH
log_half = -0.6931471805599453
epsilon = 1e-06
F32 = jnp.float32
BF16 = jnp.bfloat16


def nt_dot(a, b):
    return lax.dot_general(a, b, (((1,), (1,)), ((), ())), preferred_element_type=F32)


def tn_dot(a, b):
    return lax.dot_general(a, b, (((0,), (0,)), ((), ())), preferred_element_type=F32)


def kernel(
    heads, blocks, powers, place, tok, wsh, osh, out,
    G, tokv, gall, qbuf, wbuf, gbuf, lout, lbuf, tbuf, eout, ebuf, acc, stage,
    loc, s1, r1, s2, r2, ssib, rsib, sa, ra, sl, rl, st, rt, se, re, sx, rx,
):
    extent = tok.shape[0]
    rows = wsh.shape[2]
    half = rows // 2
    steps = heads + 2
    rem, div = lax.rem, lax.div
    s, x, zhi = lax.axis_index("seq"), lax.axis_index("tp"), lax.axis_index("rep")
    y, g, zlo, c = div(s, 4), rem(s, 4), rem(div(s, 2), 2), rem(s, 2)
    z = zhi * 2 + zlo

    def around(k, d):
        return rem(k + d, 4)

    def at_y(k):
        return {"seq": k * 4 + g}

    def at_z(k):
        return {"seq": y * 4 + rem(k, 2) * 2 + c, "rep": div(k, 2)}

    def at_g(k):
        return {"seq": y * 4 + k}

    def at_x(k):
        return {"tp": k}

    sibling = {"seq": y * 4 + zlo * 2 + 1 - c}

    barrier = pltpu.get_barrier_semaphore()

    def greet(device):
        pl.semaphore_signal(barrier, inc=1, device_id=device, device_id_type=MESH)

    def quarter(q):
        width = osh.shape[1] // 4
        return osh.at[:, pl.ds(pl.multiple_of(q * width, width), width)]

    own_copies = [
        pltpu.make_async_copy(tok, tokv, loc.at[0]),
        pltpu.make_async_copy(wsh.at[0], G.at[pl.ds(0, heads), 0, y, zlo, c, zhi], loc.at[1]),
        pltpu.make_async_copy(quarter(y), stage.at[y], loc.at[2]),
        pltpu.make_async_copy(wsh.at[1], G.at[pl.ds(0, heads), 1, y, zlo, c, zhi], loc.at[3]),
    ]
    own_copies[1].start()
    own_copies[3].start()
    own_copies[2].start()
    for d in (1, 2, 3):
        greet(at_y(around(y, d)))
        greet(at_g(around(g, d)))
        greet(at_x(around(x, d)))
    for d in (1, 3):
        greet(at_z(around(z, d)))
    pl.semaphore_wait(barrier, 11)

    def send(src, dst, ss, rs, device):
        pltpu.make_async_remote_copy(
            src_ref=src, dst_ref=dst, send_sem=ss, recv_sem=rs, device_id=device, device_id_type=MESH
        ).start()

    def got(ref, ss, rs):
        pltpu.make_async_remote_copy(
            src_ref=ref, dst_ref=ref, send_sem=ss, recv_sem=rs, device_id=sibling, device_id_type=MESH
        ).wait_recv()

    def sent(ref, ss, rs):
        pltpu.make_async_remote_copy(
            src_ref=ref, dst_ref=ref, send_sem=ss, recv_sem=rs, device_id=sibling, device_id_type=MESH
        ).wait_send()

    first_ring = ((y, at_y), (z, at_z))
    second_ring = ((z, at_z), (y, at_y))

    def unit1(m, a, k, lo=0, n=rows):
        if a == 0:
            return G.at[m, 0, k, zlo, c, zhi, pl.ds(lo, n)]
        return G.at[m, 1, y, rem(k, 2), c, div(k, 2), pl.ds(lo, n)]

    def unit2(t, a, k):
        if a == 0:
            return G.at[t, 0, :, rem(k, 2), c, div(k, 2)]
        return G.at[t, 1, k, :, c]

    def half2(t, a, k, part):
        if a == 0:
            return G.at[t, 0, pl.ds(2 * part, 2), rem(k, 2), c, div(k, 2)]
        return G.at[t, 1, k, pl.ds(part, 1), c]

    SLOTS = 4

    def slot_of(m):
        return rem(m, SLOTS)

    def reused(m, wait):
        if isinstance(m, int):
            if m >= SLOTS:
                wait()
        else:
            pl.when(m >= SLOTS)(wait)

    def first_sent(k):
        sent(G.at[0, 0, pl.ds(0, 3), :, 0, 0], s1.at[k], s1.at[k])

    def second_sent(k):
        sent(G.at[0, 0, pl.ds(0, 3)], s2.at[k], s2.at[k])

    def first_send(m):
        k0 = slot_of(m)
        reused(m, lambda: first_sent(k0))
        for a in (0, 1):
            k, at = first_ring[a]
            own = unit1(m, a, k)
            start = wsh.at[a, m] if isinstance(m, int) else own
            for d, step in ((0, 1), (1, 3)):
                send(start, own, s1.at[k0], r1.at[k0, a, d], at(around(k, step)))

    def first_pass(m):
        k0 = slot_of(m)
        for a in (0, 1):
            k, at = first_ring[a]
            for d, step in ((0, 1), (1, 3)):
                origin = around(k, 4 - step)
                got(unit1(m, a, origin), s1.at[k0], r1.at[k0, a, d])
                part = unit1(m, a, origin, d * half, half)
                send(part, part, s1.at[k0], r1.at[k0, a, 2], at(around(k, step)))

    def first_end(m):
        k0 = slot_of(m)
        for a in (0, 1):
            k, _ = first_ring[a]
            got(unit1(m, a, around(k, 2)), s1.at[k0], r1.at[k0, a, 2])

    def second_send_one(t, a, d):
        k0 = slot_of(t)
        k, at = second_ring[a]
        for n in (0, 1):
            own = half2(t, a, k, (d + n) % 2)
            send(own, own, s2.at[k0], r2.at[k0, a, d + 3 * n], at(around(k, 3 if d else 1)))

    def second_pass_one(t, a, d):
        k0 = slot_of(t)
        k, at = second_ring[a]
        step = 3 if d else 1
        origin = around(k, 4 - step)
        part = half2(t, a, origin, d)
        got(part, s2.at[k0], r2.at[k0, a, d])
        send(part, part, s2.at[k0], r2.at[k0, a, 2], at(around(k, step)))

    def second_end(t):
        k0 = slot_of(t)
        for a in (1, 0):
            k, _ = second_ring[a]
            for d in (0, 1):
                got(half2(t, a, k, d), s2.at[k0], r2.at[k0, a, 3 + d])
            got(unit2(t, a, around(k, 2)), s2.at[k0], r2.at[k0, a, 2])

    def share_sent(k):
        sent(G.at[0, :, :, :, c], ssib.at[k], ssib.at[k])

    def share(t):
        k0 = slot_of(t)
        reused(t, lambda: share_sent(k0))
        mine = G.at[t, :, :, :, c]
        send(mine, mine, ssib.at[k0], rsib.at[k0], sibling)

    def shared(t):
        k0 = slot_of(t)
        got(G.at[t, :, :, :, 1 - c], ssib.at[k0], rsib.at[k0])

    def out_unit(k, q):
        return G.at[heads + div(k, 2), rem(k, 2), q, zlo, c, zhi]

    def regroup_y():
        for d in (1, 2, 3):
            q = around(y, d)
            send(quarter(q), stage.at[y], sa.at[0], ra.at[0], at_y(q))

    def regroup_x():
        own_copies[2].wait()
        got(stage.at[pl.ds(0, 3)], sa.at[0], ra.at[0])
        pltpu.make_async_copy(stage.at[x], out_unit(x, y), loc.at[2]).start()
        for d in (1, 2, 3):
            k = around(x, d)
            send(stage.at[k], out_unit(x, y), sa.at[1], ra.at[1], at_x(k))

    def regrouped():
        pltpu.make_async_copy(stage.at[x], out_unit(x, y), loc.at[2]).wait()
        got(stage.at[pl.ds(0, 3)], sa.at[1], ra.at[1])

    first_send(0)
    first_send(1)
    first_send(2)
    regroup_y()
    own_copies[0].start()
    first_pass(0)
    own_copies[1].wait()
    own_copies[3].wait()
    first_pass(1)
    first_end(0)
    for a in (0, 1):
        for d in (0, 1):
            second_send_one(0, a, d)
    first_pass(2)
    first_send(3)
    regroup_x()
    acc[...] = jnp.zeros_like(acc)
    own_copies[0].wait()

    edge = place[0] - s * extent
    crossing = div(place[0], extent)
    base = y * 4

    def rate_of(h):
        return (log_half / (extent * blocks)) * jnp.left_shift(1, powers[h]).astype(F32)

    def left(h, k, p):
        clear = (k < p) & jnp.logical_not((k < crossing) & (crossing < p))
        span = (extent * jnp.maximum(p - 1 - k, 0)).astype(F32)
        share = jnp.exp(jnp.full((8, HDIM), rate_of(h) * span, F32))[:1]
        return jnp.where(clear, share, 0.0)

    down = lax.broadcasted_iota(jnp.int32, (extent, HDIM), 0)
    BR = 256
    QR = HDIM // 4

    def blocks_sent(sem):
        sent(lbuf.at[0, pl.ds(0, 3)], sem, sem)

    def gated_sent(k):
        sent(gall.at[pl.ds(0, 3), 0], sx.at[k], sx.at[k])

    def project(h):
        slot = rem(h, 4)
        rate = rate_of(h)
        panel = G[h, 0].reshape(-1, 2 * HDIM)
        u = jnp.dot(tokv[...], panel, preferred_element_type=F32)
        down_f = down.astype(F32)
        grow = jnp.exp(rate * down_f)
        shrink = jnp.exp(-rate * down_f)
        uq, uk = u[:, :HDIM], u[:, HDIM:]
        q = ((uq / (1.0 + jnp.exp(-uq))) * (HDIM ** -0.5) * grow).astype(BF16)
        kf = (uk / (1.0 + jnp.exp(-uk))) * shrink
        k = kf.astype(BF16)
        kept = jnp.where((down >= edge) | (edge >= extent), kf, 0.0).astype(BF16)
        panel = G[h, 1].reshape(-1, 2 * HDIM)
        u = jnp.dot(tokv[...], panel, preferred_element_type=F32)
        v = u[:, :HDIM].astype(BF16)
        gbuf[slot] = 1.0 / (1.0 + jnp.exp(-u[:, HDIM:]))
        qbuf[slot] = q
        k0 = slot_of(h)
        reused(h, lambda: blocks_sent(sl.at[k0]))
        added = (tn_dot(kept, v) * jnp.exp(jnp.full((8, HDIM), rate * (extent - 1), F32))[:1]).astype(BF16)
        lout[k0] = added
        lbuf[h, g] = lout[k0, pl.ds(g * QR, QR)]
        for d in (1, 2, 3):
            to = around(g, d)
            send(lout.at[k0, pl.ds(to * QR, QR)], lbuf.at[h, g], sl.at[k0], rl.at[k0], at_g(to))
        for lo in range(0, extent, BR):
            hi = lo + BR
            scores = nt_dot(q[lo:hi], k[:hi])
            i = lax.broadcasted_iota(jnp.int32, (BR, hi), 0) + lo
            j = lax.broadcasted_iota(jnp.int32, (BR, hi), 1)
            keep = (j <= i) & (j >= jnp.where(i >= edge, edge, 0))
            scores = jnp.where(keep, scores, 0.0).astype(BF16)
            wbuf[slot, pl.ds(lo, BR)] = jnp.dot(scores, v[:hi], preferred_element_type=F32)

    def gather_states(h):
        k0 = slot_of(h)
        got(lbuf.at[h, pl.ds(0, 3)], sl.at[k0], rl.at[k0])
        total = jnp.zeros((QR, HDIM), F32)
        for k in range(4):
            total += left(h, base + k, base + 4) * lbuf[h, k].astype(F32)
        reused(h, lambda: blocks_sent(st.at[k0]))
        tbuf[h, y] = total.astype(BF16)
        for d in (1, 2, 3):
            own = tbuf.at[h, y]
            send(own, own, st.at[k0], rt.at[k0], at_y(around(y, d)))

    def spread_states(h):
        k0 = slot_of(h)
        got(tbuf.at[h, pl.ds(0, 3)], st.at[k0], rt.at[k0])
        reused(h, lambda: blocks_sent(se.at[k0]))
        for p in range(4):
            state = jnp.zeros((QR, HDIM), F32)
            for k in range(4):
                if k < p:
                    state += left(h, base + k, base + p) * lbuf[h, k].astype(F32)
                state += left(h, 4 * k + 3, base + p) * tbuf[h, k].astype(F32)
            eout[k0, p] = state.astype(BF16)
        ebuf[h, g] = eout[k0, g]
        for d in (1, 2, 3):
            k = around(g, d)
            send(eout.at[k0, k], ebuf.at[h, g], se.at[k0], re.at[k0], at_g(k))

    def finish(h):
        slot = rem(h, 4)
        k0 = slot_of(h)
        got(ebuf.at[h, pl.ds(0, 3)], se.at[k0], re.at[k0])
        state = ebuf[h].reshape(HDIM, HDIM)
        once = jnp.exp(jnp.full((8, HDIM), rate_of(h), F32))[:1]
        use = jnp.where((down < edge) | (edge < 0), once, 0.0)
        across = jnp.dot(qbuf[slot], state, preferred_element_type=F32)
        attended = wbuf[slot] + across * use
        square = jnp.mean(attended * attended, axis=-1, keepdims=True)
        gall[x, h] = (attended * lax.rsqrt(square + epsilon) * gbuf[slot]).astype(BF16)
        reused(h, lambda: gated_sent(k0))
        for n in (0, 1):
            for d, step in ((0, 1), (1, 3)):
                own = half_rows(x, h, (d + n) % 2)
                send(own, own, sx.at[k0], rx.at[k0, d + 3 * n], at_x(around(x, step)))

    def half_rows(k, h, d):
        return gall.at[k, h, pl.ds(d * (extent // 2), extent // 2)]

    def pass_gated(h):
        k0 = slot_of(h)
        for d, step in ((0, 1), (1, 3)):
            origin = around(x, 4 - step)
            part = half_rows(origin, h, d)
            got(part, sx.at[k0], rx.at[k0, d])
            send(part, part, sx.at[k0], rx.at[k0, 2], at_x(around(x, step)))

    def end_gated(h):
        k0 = slot_of(h)
        for d in (0, 1):
            got(half_rows(x, h, d), sx.at[k0], rx.at[k0, 3 + d])
        got(gall.at[around(x, 2), h], sx.at[k0], rx.at[k0, 2])

    def emit(i, q):
        panel = jnp.concatenate(
            [G[heads + i, a, q].reshape(-1, 2 * HDIM) for a in (0, 1)], axis=1
        )
        for lo in range(0, extent, BR):
            left = jnp.concatenate(
                [gall[2 * i + a, 2 * q + b, pl.ds(lo, BR)] for a in (0, 1) for b in (0, 1)], axis=1
            )
            acc[pl.ds(lo, BR)] += nt_dot(left, panel)

    def turn(n, carry):
        t = n - 1

        def when(lag, count):
            return pl.when((t >= lag) & (t - lag < count))

        @pl.when(t + 2 < steps)
        def _():
            first_end(t + 2)
            reused(t + 2, lambda: second_sent(slot_of(t + 2)))

        def ring(a, d):
            @when(-1, steps)
            def _():
                second_pass_one(t + 1, a, d)

        def own(a, d):
            @pl.when(t + 2 < steps)
            def _():
                second_send_one(t + 2, a, d)

        for d in (0, 1):
            ring(0, d)
            own(0, d)
        ring(1, 0)
        ring(1, 1)
        @when(1, heads)
        def _():
            gather_states(t - 1)
        own(1, 0)
        own(1, 1)
        @when(2, heads)
        def _():
            finish(t - 2)
        @when(0, steps)
        def _():
            shared(t)
        @when(0, heads)
        def _():
            project(t)
        @when(-1, steps)
        def _():
            second_end(t + 1)
        @when(-1, steps)
        def _():
            share(t + 1)
        @pl.when(t + 4 < steps)
        def _():
            first_pass(t + 4)
        @pl.when(t + 5 == heads)
        def _():
            regrouped()
        @pl.when(t + 5 < steps)
        def _():
            first_send(t + 5)
        @when(1, heads)
        def _():
            spread_states(t - 1)
        @pl.when(t == heads + 1)
        def _():
            lax.fori_loop(0, 4, lambda n, carry: (emit(div(n, 2), rem(n, 2)), carry)[1], 0)
        @when(2, heads)
        def _():
            pass_gated(t - 2)
        @when(3, heads)
        def _():
            end_gated(t - 3)
        return carry

    lax.fori_loop(0, steps + 1, turn, 0)

    def both(q):
        lax.fori_loop(0, 2, lambda i, carry: (emit(i, q), carry)[1], 0)

    both(2)
    end_gated(heads - 1)
    both(3)
    out[...] = acc[...].astype(out.dtype)

    for k in range(SLOTS):
        first_sent(k)
        second_sent(k)
        share_sent(k)
        blocks_sent(sl.at[k])
        blocks_sent(st.at[k])
        blocks_sent(se.at[k])
        gated_sent(k)
    for k in range(2):
        sent(stage.at[pl.ds(0, 3)], sa.at[k], sa.at[k])


def local(tokens, in_panels, out_panel, decay_power, boundary):
    slab_rows = tokens[0]
    extent, depth = slab_rows.shape
    seq_count = lax.axis_size("seq")
    heads = decay_power.shape[0]
    rows = in_panels.shape[0]
    flat = lax.optimization_barrier(in_panels.reshape(rows, 4 * heads * HDIM))
    tiles = flat.reshape(rows, 4 * heads, HDIM).transpose(1, 0, 2)
    tiles = tiles.reshape(2, 2, heads, rows, HDIM)
    shard = jnp.concatenate([tiles[:, 0], tiles[:, 1]], axis=-1)
    out_shard = out_panel.T

    any_space = pl.BlockSpec(memory_space=pl.ANY)
    smem = pl.BlockSpec(memory_space=pltpu.SMEM)
    dma = pltpu.SemaphoreType.DMA
    steps = heads + 2
    columns = out_panel.shape[1] * 8
    result = pl.pallas_call(
        functools.partial(kernel, heads, seq_count),
        out_shape=jax.ShapeDtypeStruct((extent, columns), BF16),
        in_specs=[smem, smem, any_space, any_space, any_space],
        out_specs=pl.BlockSpec(memory_space=pltpu.VMEM),
        scratch_shapes=[
            pltpu.VMEM((steps, 2, 4, 2, 2, 2, rows, 2 * HDIM), BF16),
            pltpu.VMEM((extent, depth), BF16),
            pltpu.VMEM((4, heads, extent, HDIM), BF16),
            pltpu.VMEM((4, extent, HDIM), BF16),
            pltpu.VMEM((4, extent, HDIM), F32),
            pltpu.VMEM((4, extent, HDIM), F32),
            pltpu.VMEM((4, HDIM, HDIM), BF16),
            pltpu.VMEM((heads, 4, HDIM // 4, HDIM), BF16),
            pltpu.VMEM((heads, 4, HDIM // 4, HDIM), BF16),
            pltpu.VMEM((4, 4, HDIM // 4, HDIM), BF16),
            pltpu.VMEM((heads, 4, HDIM // 4, HDIM), BF16),
            pltpu.VMEM((extent, columns), F32),
            pltpu.VMEM((4, out_panel.shape[1], out_panel.shape[0] // 4), BF16),
            dma((4,)),
            dma((4,)),
            dma((4, 2, 3)),
            dma((4,)),
            dma((4, 2, 5)),
            dma((4,)),
            dma((4,)),
            dma((2,)),
            dma((2,)),
            dma((4,)),
            dma((4,)),
            dma((4,)),
            dma((4,)),
            dma((4,)),
            dma((4,)),
            dma((4,)),
            dma((4, 5)),
        ],
        compiler_params=pltpu.CompilerParams(
            collective_id=0, has_side_effects=True, vmem_limit_bytes=60 * 1024 * 1024
        ),
        cost_estimate=pl.CostEstimate(
            flops=2 * extent * depth * 4 * heads * HDIM, bytes_accessed=8_000_000, transcendentals=0
        ),
    )(decay_power, boundary, slab_rows, shard, out_shard)
    return result[None]


def solution(mesh):
    return jax.shard_map(
        local,
        mesh=mesh,
        in_specs=(
            P("rep", "seq", None),
            P(("seq", "rep"), None, "tp"),
            P("tp", ("seq", "rep")),
            P("tp"),
            P("rep"),
        ),
        out_specs=P("rep", "seq", "tp"),
        check_vma=False,
    )
```
